256 devices in a mesh: mz: 8 (over z), px: 32 (over x, y, core).
Axes of the slice: x: 4, y: 4, z: 8, core: 2. Of those that a mesh axis runs over, the one named last changes fastest.
Arguments:
- spectra: float32 [12288, 12288], P('px', 'mz'), may hold values from 0 to 10
- w_factor: float32 [48, 12288], P(None, ('px', 'mz')), may hold values from 0.05 to 1
- h_factor: float32 [48, 12288], P(None, ('mz', 'px')), may hold values from 0.05 to 1
Outputs:
- w_final: float32 [48, 12288], P(None, ('px', 'mz'))
- h_final: float32 [48, 12288], P(None, ('mz', 'px'))
- misfit: float32 [12288], P(('px', 'mz'))
The draws below stay inside these ranges and needn't reach their ends.
All inputs are finite; a program needn't handle non-finite values.
Results may differ from the reference program's by a relative error of at most 0.0001.
Values sent between devices are 32-bit elements; how exact they have to be, the bound alone decides.
A program may use at most 64 MiB of HBM per device.

```python
import math
import jax
import jax.numpy as jnp
from jax import lax

RANK = 48
MZBINS = 12288
PIX_DEV = 384
ITERS = 3
PIXELS = 12288


def block_levels(stream_key, extent, shards, smallest, high):
    level, own = 1.0, jax.random.fold_in(stream_key, 6)
    for position, blocks in shards:
        draws = jnp.exp(jax.random.uniform(jax.random.fold_in(own, position), (blocks,), jnp.float32, smallest / len(shards), high / len(shards)))
        level = level * jnp.repeat(draws, extent[position] // blocks).reshape([-1 if axis == position else 1 for axis in range(len(extent))])
    return level


def setup_inputs(seed: int = 0) -> dict:
    key_of = jax.random.split(jax.random.key(seed), 4)
    return {
        "spectra": jnp.clip(10.0 * jax.random.uniform(key_of[0], (PIXELS, MZBINS), jnp.float32) ** block_levels(key_of[0], (PIXELS, MZBINS), ((0, 32), (1, 8)), -0.2, 0.2), 0.0, 10.0),
        "w_factor": jnp.clip(jnp.exp(math.log(1.0) - 2.9957323 * jax.random.uniform(key_of[1], (RANK, PIXELS), jnp.float32) ** block_levels(key_of[1], (RANK, PIXELS), ((1, 256),), -0.2, 0.2)), 0.05, 1.0),
        "h_factor": jnp.clip(jnp.exp(math.log(1.0) - 2.9957323 * jax.random.uniform(key_of[2], (RANK, MZBINS), jnp.float32) ** block_levels(key_of[2], (RANK, MZBINS), ((1, 256),), -0.2, 0.2)), 0.05, 1.0),
    }


def matmul(left, right):
    return jnp.dot(left, right, preferred_element_type=jnp.float32, precision=lax.Precision.HIGHEST)


def reference(spectra, w_factor, h_factor):
    loadings = w_factor
    components = h_factor
    for iteration in range(ITERS):
        components = components * matmul(loadings, spectra) / matmul(matmul(loadings, loadings.T), components)
        loadings = loadings * matmul(components, spectra.T) / matmul(matmul(components, components.T), loadings)
    blocks = spectra.reshape(PIXELS // PIX_DEV, PIX_DEV, MZBINS)
    load_blocks = loadings.T.reshape(PIXELS // PIX_DEV, PIX_DEV, RANK)

    def block_error(pair):
        data, load = pair
        diff = data - matmul(load, components)
        return jnp.sum(diff * diff, axis=1)

    misfit = lax.map(block_error, (blocks, load_blocks)).reshape(PIXELS)
    return loadings, components, misfit
```

```python
import jax
import jax.numpy as jnp
from jax import lax
from jax.experimental import pallas as pl
from jax.experimental.pallas import tpu as pltpu
from jax.sharding import PartitionSpec as P

ITERS = 3
RANK = 48
GROUPS = 8
ROWS = RANK // GROUPS
PADDED = 8 * GROUPS
HALF = 384
WIDE = 2 * HALF
PIECE = 48
CHIPS = 16
DEPTH = 8
F32 = jnp.float32
BF16 = jnp.bfloat16
MESH = pl.DeviceIdType.MESH


def split(value):
    high = value.astype(BF16)
    return high, (value - high.astype(F32)).astype(BF16)


def dot(left, right, dims, precision=None):
    return lax.dot_general(left, right, (dims, ((), ())), precision=precision, preferred_element_type=F32)


NN = ((1,), (0,))
NT = ((1,), (1,))
TN = ((0,), (0,))


def pack(piece_ref, packed_ref):
    pad = jnp.zeros((24, 64 - PIECE), F32)
    packed_ref[...] = jnp.concatenate([piece_ref[0:24, :], pad, piece_ref[24:48, :], pad], axis=1)


def unpack(packed, flat_ref):
    lane = lax.broadcasted_iota(jnp.int32, (24, 128), 1)
    for top, back in ((0, 0), (24, 64)):
        r = [pltpu.roll(value, (PIECE * p - back) % 128, 1) for p, value in enumerate(packed)]
        rows = pl.ds(top, 24)
        flat_ref[rows, 0:128] = jnp.where(lane < 48, r[0], jnp.where(lane < 96, r[1], r[2]))
        flat_ref[rows, 128:256] = jnp.where(
            lane < 16, r[2], jnp.where(lane < 64, r[3], jnp.where(lane < 112, r[4], r[5]))
        )
        flat_ref[rows, 256:384] = jnp.where(lane < 32, r[5], jnp.where(lane < 80, r[6], r[7]))


def kernel(
    x_hbm, w_in, h_in, w_out, h_out, m_out,
    x32, xh, xl, wcur, hcur, wst, hst, flat,
    wpk, hpk, wpieces, wsib, hpieces, hall,
    hs_send, hs_recv, h_new, h_gath, c_num, c_recv, z_send, z_recv, w_new, w_gath,
    rows8, h_pick, h_pick_sib, m_row, m_sib, m_send, m_recv, astack, bstack,
    local_sem, start_send, start_recv, loop_send, loop_recv, end_send, end_recv,
):
    px = lax.axis_index("px")
    z = lax.axis_index("mz")
    chip = lax.div(px, 2)
    core = lax.rem(px, 2)
    other = 1 - core
    sibling = {"px": px + 1 - 2 * core}

    def chip_at(step):
        return lax.rem(chip + step, CHIPS)

    def depth_at(step):
        return lax.rem(z + step, DEPTH)

    def remote(source, target, send, recv, device):
        return pltpu.make_async_remote_copy(
            src_ref=source, dst_ref=target, send_sem=send, recv_sem=recv, device_id=device, device_id_type=MESH
        )

    def settle(ref, sem):
        pltpu.make_async_copy(ref, ref, sem).wait()

    own_x = pltpu.make_async_copy(x_hbm.at[:, pl.ds(pl.multiple_of(core * WIDE, 128), WIDE)], x32.at[core], local_sem)
    own_x.start()

    barrier = pltpu.get_barrier_semaphore()
    for step in range(1, CHIPS):
        pl.semaphore_signal(barrier, inc=1, device_id={"px": 2 * chip_at(step) + core}, device_id_type=MESH)
    for step in range(1, DEPTH):
        pl.semaphore_signal(barrier, inc=1, device_id={"mz": depth_at(step)}, device_id_type=MESH)
    pl.semaphore_signal(barrier, inc=1, device_id=sibling, device_id_type=MESH)

    pack(w_in, wpk)
    pack(h_in, hpk)
    wcur[...] = jnp.zeros_like(wcur)
    hcur[...] = jnp.zeros_like(hcur)
    rows8[...] = jnp.zeros_like(rows8)
    wpieces[z] = wpk[...]
    hpieces[chip] = hpk[...]

    pl.semaphore_wait(barrier, CHIPS + DEPTH - 1)

    for step in range(1, DEPTH):
        remote(wpk, wpieces.at[z], start_send.at[0], start_recv.at[0], {"mz": depth_at(step)}).start()
    sib_x = remote(
        x_hbm.at[:, pl.ds(pl.multiple_of(other * WIDE, 128), WIDE)], x32.at[core], start_send.at[1], start_recv.at[1], sibling
    )
    sib_x.start()
    for step in range(1, CHIPS):
        remote(hpk, hpieces.at[chip], start_send.at[2], start_recv.at[2], {"px": 2 * chip_at(step) + core}).start()

    def convert(which):
        def body(i, _):
            rows = pl.ds(pl.multiple_of(i * 64, 64), 64)
            high, low = split(x32[which, rows, :])
            xh[which, rows, :] = high
            xl[which, rows, :] = low
            return 0

        lax.fori_loop(0, HALF // 64, body, 0)

    def spread(target, which):
        for g in range(GROUPS):
            target[which, g, 0:ROWS, :] = flat[ROWS * g : ROWS * g + ROWS, :]

    own_x.wait()
    convert(core)
    settle(wpieces.at[pl.ds(0, DEPTH - 1)], start_recv.at[0])
    sib_w = remote(wpieces, wsib, start_send.at[3], start_recv.at[3], sibling)
    sib_w.start()
    unpack([wpieces[p] for p in range(DEPTH)], flat)
    spread(wcur, core)
    settle(hpieces.at[pl.ds(0, CHIPS - 1)], start_recv.at[2])
    sib_h = remote(hpieces.at[pl.ds(8 * other, 8)], hall.at[core], start_send.at[4], start_recv.at[4], sibling)
    sib_h.start()
    sib_w.wait_recv()
    unpack([wsib[p] for p in range(DEPTH)], flat)
    spread(wcur, other)
    sib_x.wait_recv()
    convert(other)
    for j in range(8):
        hall[core, j] = hpieces[8 * core + j]
    sib_h.wait_recv()
    for part in range(2):
        unpack([hall[p % 2, p // 2] for p in range(8 * part, 8 * part + 8)], flat)
        spread(hcur, part)
    settle(wpieces.at[pl.ds(0, DEPTH - 1)], start_send.at[0])
    settle(hpieces.at[pl.ds(0, CHIPS - 1)], start_send.at[2])
    sib_x.wait_send()
    sib_w.wait_send()
    sib_h.wait_send()

    def stack(cur, target):
        for part in range(2):
            high, low = split(cur[part].reshape(PADDED, HALF))
            target[0:PADDED, part * HALF : part * HALF + HALF] = high
            target[PADDED : 2 * PADDED, part * HALF : part * HALF + HALF] = low

    def gram(stacked):
        both = dot(stacked[...], stacked[...], NT)
        rows = both[0:PADDED] + both[PADDED : 2 * PADDED]
        return rows + pltpu.roll(rows, 64, 1)

    def three(stacked, high, low, dims):
        first = dot(stacked[...], high, dims)
        return first[0:PADDED] + first[PADDED : 2 * PADDED] + dot(stacked[0:PADDED, :], low, dims)

    def updated(total, cur, part, group):
        rows8[0:ROWS, :] = total
        below = dot(rows8[:, HALF : HALF + PADDED], cur[part].reshape(PADDED, HALF), NN, lax.Precision.HIGHEST)
        return cur[part, group, 0:ROWS, :] * total[:, 0:HALF] / below[0:ROWS]

    stack(wcur, wst)
    owner_part = lax.div(chip, 8)
    owner_group = lax.rem(chip, 8)

    def iteration(it, _):
        product = gram(wst).reshape(GROUPS, 8, 128)[:, 0:ROWS, :]
        for part in range(2):
            columns = slice(part * HALF, part * HALF + HALF)
            high = xh[:, :, columns].reshape(WIDE, HALF)
            low = xl[:, :, columns].reshape(WIDE, HALF)
            above = three(wst, high, low, NN)
            hs_send[8 * part : 8 * part + 8, :, 0:HALF] = above.reshape(GROUPS, 8, HALF)[:, 0:ROWS, :]
            hs_send[8 * part : 8 * part + 8, :, HALF : HALF + 128] = product
        for step in range(1, CHIPS):
            to = chip_at(step)
            remote(
                hs_send.at[to], hs_recv.at[it, chip], loop_send.at[it, 0], loop_recv.at[it, 0], {"px": 2 * to + core}
            ).start()
        hs_recv[it, chip] = hs_send[chip]
        settle(hs_recv.at[it, pl.ds(0, CHIPS - 1)], loop_recv.at[it, 0])
        total = jnp.sum(hs_recv[it], axis=0)
        fresh = updated(total, hcur, owner_part, owner_group)
        h_new[...] = fresh
        for step in range(1, CHIPS):
            to = chip_at(step)
            remote(
                h_new, h_gath.at[it, chip], loop_send.at[it, 1], loop_recv.at[it, 1], {"px": 2 * to + core}
            ).start()
        h_gath[it, chip] = fresh
        settle(hs_recv.at[it, pl.ds(0, CHIPS - 1)], loop_send.at[it, 0])
        settle(h_gath.at[it, pl.ds(0, CHIPS - 1)], loop_recv.at[it, 1])
        for part in range(2):
            hcur[part, :, 0:ROWS, :] = h_gath[it, 8 * part : 8 * part + 8]
        stack(hcur, hst)
        settle(h_gath.at[it, pl.ds(0, CHIPS - 1)], loop_send.at[it, 1])

        product = gram(hst).reshape(GROUPS, 8, 128)[:, 0:ROWS, :]
        c_num[other, :, :, HALF : HALF + 128] = product
        c_num[other, :, :, 0:HALF] = three(hst, xh[other], xl[other], NT).reshape(GROUPS, 8, HALF)[:, 0:ROWS, :]
        across = remote(c_num.at[other], c_recv.at[it], loop_send.at[it, 2], loop_recv.at[it, 2], sibling)
        across.start()
        c_num[core, :, :, HALF : HALF + 128] = product
        c_num[core, :, :, 0:HALF] = three(hst, xh[core], xl[core], NT).reshape(GROUPS, 8, HALF)[:, 0:ROWS, :]
        across.wait()
        z_send[...] = c_num[core] + c_recv[it]
        for step in range(1, DEPTH):
            to = depth_at(step)
            remote(z_send.at[to], z_recv.at[it, z], loop_send.at[it, 3], loop_recv.at[it, 3], {"mz": to}).start()
        z_recv[it, z] = z_send[z]
        settle(z_recv.at[it, pl.ds(0, DEPTH - 1)], loop_recv.at[it, 3])
        fresh = updated(jnp.sum(z_recv[it], axis=0), wcur, core, z)
        w_new[...] = fresh
        for step in range(1, DEPTH):
            to = depth_at(step)
            remote(w_new, w_gath.at[it, core, z], loop_send.at[it, 4], loop_recv.at[it, 4], {"mz": to}).start()
        w_gath[it, core, z] = fresh
        settle(z_recv.at[it, pl.ds(0, DEPTH - 1)], loop_send.at[it, 3])
        settle(w_gath.at[it, core, pl.ds(0, DEPTH - 1)], loop_recv.at[it, 4])
        across = remote(
            w_gath.at[it, core], w_gath.at[it, core], loop_send.at[it, 5], loop_recv.at[it, 5], sibling
        )
        across.start()
        settle(w_gath.at[it, core, pl.ds(0, DEPTH - 1)], loop_send.at[it, 4])
        across.wait()
        for part in range(2):
            wcur[part, :, 0:ROWS, :] = w_gath[it, part]
        stack(wcur, wst)
        return 0

    lax.fori_loop(0, ITERS, iteration, 0)

    def pick(value, start, count):
        row = lax.broadcasted_iota(jnp.int32, (count, 128), 0)
        column = lax.broadcasted_iota(jnp.int32, (count, 128), 1)
        chosen = (row == column + start).astype(F32)
        return dot(value, chosen, NN, lax.Precision.HIGHEST)

    def bins_of(which):
        start = PIECE * (2 * owner_group + which)
        total = pick(hcur[0].reshape(PADDED, HALF), start, HALF)
        total += pick(hcur[1].reshape(PADDED, HALF), start - HALF, HALF)
        return total.reshape(GROUPS, 8, 128)

    h_pick[0] = bins_of(other)
    across = remote(h_pick.at[0], h_pick_sib, end_send.at[0], end_recv.at[0], sibling)
    across.start()
    h_pick[1] = bins_of(core)
    picked = pick(wcur[core].reshape(PADDED, HALF), PIECE * z, HALF)
    for g in range(GROUPS):
        w_out[ROWS * g : ROWS * g + ROWS, :] = picked[8 * g : 8 * g + ROWS, 0:PIECE]
    across.wait()
    h_block = jnp.where(owner_part == core, h_pick[1], h_pick_sib[...])
    for g in range(GROUPS):
        h_out[ROWS * g : ROWS * g + ROWS, :] = h_block[g, 0:ROWS, 0:PIECE]

    for t in range(4):
        rows = slice(t * PADDED, t * PADDED + PADDED)
        astack[rows, :] = wst[(t % 2) * PADDED : (t % 2) * PADDED + PADDED, :]
        bstack[rows, :] = hst[(t // 2) * PADDED : (t // 2) * PADDED + PADDED, :]
    ones = jnp.ones((8, 128), F32)
    for part in range(2):
        for i in range(3):
            columns = slice(part * HALF + i * 128, part * HALF + i * 128 + 128)
            model = dot(astack[:, columns], bstack[...], TN)
            diff = x32[part, i * 128 : i * 128 + 128, :] - model
            square = diff * diff
            folded = square[:, 0:128]
            for j in range(1, 6):
                folded += square[:, 128 * j : 128 * j + 128]
            m_row[part, 0:1, i * 128 : i * 128 + 128] = dot(ones, folded, NT, lax.Precision.HIGHEST)[0:1]
    across = remote(m_row.at[other], m_sib, end_send.at[1], end_recv.at[1], sibling)
    across.start()
    across.wait()
    m_send[...] = m_row[core] + m_sib[...]
    for step in range(1, DEPTH):
        remote(m_send, m_recv.at[z], end_send.at[2], end_recv.at[2], {"mz": depth_at(step)}).start()
    m_recv[z] = m_send[...]
    settle(m_recv.at[pl.ds(0, DEPTH - 1)], end_recv.at[2])
    settle(m_recv.at[pl.ds(0, DEPTH - 1)], end_send.at[2])
    error = jnp.broadcast_to(jnp.sum(m_recv[...], axis=0), (8, HALF))
    m_out[...] = pick(error, PIECE * z, HALF)[0:1, 0:PIECE]


def per_device(spectra, w_factor, h_factor):
    dma = pltpu.SemaphoreType.DMA
    scratch = [
        ((2, HALF, WIDE), F32),
        ((2, HALF, WIDE), BF16),
        ((2, HALF, WIDE), BF16),
        ((2, GROUPS, 8, HALF), F32),
        ((2, GROUPS, 8, HALF), F32),
        ((2 * PADDED, WIDE), BF16),
        ((2 * PADDED, WIDE), BF16),
        ((RANK, HALF), F32),
        ((24, 128), F32),
        ((24, 128), F32),
        ((DEPTH, 24, 128), F32),
        ((DEPTH, 24, 128), F32),
        ((CHIPS, 24, 128), F32),
        ((2, 8, 24, 128), F32),
        ((CHIPS, ROWS, HALF + 128), F32),
        ((ITERS, CHIPS, ROWS, HALF + 128), F32),
        ((ROWS, HALF), F32),
        ((ITERS, CHIPS, ROWS, HALF), F32),
        ((2, GROUPS, ROWS, HALF + 128), F32),
        ((ITERS, GROUPS, ROWS, HALF + 128), F32),
        ((GROUPS, ROWS, HALF + 128), F32),
        ((ITERS, DEPTH, ROWS, HALF + 128), F32),
        ((ROWS, HALF), F32),
        ((ITERS, 2, DEPTH, ROWS, HALF), F32),
        ((8, HALF + 128), F32),
        ((2, GROUPS, 8, 128), F32),
        ((GROUPS, 8, 128), F32),
        ((2, 1, HALF), F32),
        ((1, HALF), F32),
        ((1, HALF), F32),
        ((DEPTH, 1, HALF), F32),
        ((4 * PADDED, WIDE), BF16),
        ((4 * PADDED, WIDE), BF16),
    ]
    w_final, h_final, misfit = pl.pallas_call(
        kernel,
        out_shape=(
            jax.ShapeDtypeStruct((RANK, PIECE), F32),
            jax.ShapeDtypeStruct((RANK, PIECE), F32),
            jax.ShapeDtypeStruct((1, PIECE), F32),
        ),
        in_specs=[
            pl.BlockSpec(memory_space=pl.ANY),
            pl.BlockSpec(memory_space=pltpu.VMEM),
            pl.BlockSpec(memory_space=pltpu.VMEM),
        ],
        out_specs=(pl.BlockSpec(memory_space=pltpu.VMEM),) * 3,
        scratch_shapes=[pltpu.VMEM(shape, dtype) for shape, dtype in scratch]
        + [dma, dma((5,)), dma((5,)), dma((ITERS, 6)), dma((ITERS, 6)), dma((3,)), dma((3,))],
        compiler_params=pltpu.CompilerParams(
            collective_id=0, has_side_effects=True, vmem_limit_bytes=40 * 1024 * 1024
        ),
    )(spectra, w_factor, h_factor)
    return w_final, h_final, misfit.reshape(PIECE)


def solution(mesh):
    in_specs = (P("px", "mz"), P(None, ("px", "mz")), P(None, ("mz", "px")))
    out_specs = (P(None, ("px", "mz")), P(None, ("mz", "px")), P(("px", "mz")))
    return jax.shard_map(
        per_device, mesh=mesh, in_specs=in_specs, out_specs=out_specs, check_vma=False
    )
```
